32 devices in a mesh: grp: 2 (over y), unit: 4 (over z), period: 2 (over x), rep: 2 (over core).
Axes of the slice: x: 2, y: 2, z: 4, core: 2. Of those that a mesh axis runs over, the one named last changes fastest.
Arguments:
- panel_data: bfloat16 [9216, 2560], P(('grp', 'unit'), ('period', 'rep')), parts along dimension 0, may hold values from -12 to 12
- observed: int32 [9216, 2560], P(('grp', 'unit'), ('period', 'rep')), parts along dimension 0, may hold values 0 or 1
- unit_factors: float32 [9216, 32], P(('grp', 'unit', 'period', 'rep')), parts along dimension 0, may hold values from -6 to 6
- period_factors: float32 [5120, 32], P(('grp', 'period', 'rep')), parts along dimension 0, may hold values from -6 to 6
Outputs:
- unit_result: float32 [9216, 32], P(('grp', 'unit', 'period', 'rep')), parts along dimension 0
- period_result: float32 [5120, 32], P(('grp', 'period', 'rep')), parts along dimension 0
The draws below stay inside these ranges and needn't reach their ends.
There are 2 independent parts, one for each index of `grp`. The reference program is written for one: setup_inputs(seed, part) draws one part's arguments, and reference() takes and returns one part's arrays. A program takes and returns all parts, laid end to end along the dimension named above; each array names one. Nothing has to cross between parts.
All inputs are finite; a program needn't handle non-finite values. No bound on the sum of `observed` on one device may be relied on, other than what follows from the above.
Results may differ from the reference program's by a relative error of at most 0.0039.
Values may be sent and summed in bfloat16 or wider, within the bound.
No kernel may reach another device: no remote copies, remote signals or barrier semaphores. Data moves between devices by JAX's collectives and lax.ppermute only.
A program may use at most 64 MiB of HBM per device.

```python
import math
import jax
import jax.numpy as jnp
from jax import lax

RANK = 32
ITERS = 2
UNITS = 4608
PERIODS = 2560


def place_ends(result, stream_key, low, top_value):
    place = [jax.random.randint(jax.random.fold_in(stream_key, axis), (), 0, length) for axis, length in enumerate(result.shape)]
    main_axis = result.shape.index(max(result.shape))
    neighbour = place[:main_axis] + [(place[main_axis] + 1) % result.shape[main_axis]] + place[main_axis + 1:]
    return result.at[tuple(place)].set(low).at[tuple(neighbour)].set(top_value)


def level_of(rng, dims, shards, low, top_value):
    gain, own = 1.0, jax.random.fold_in(rng, 6)
    for dim, parts in shards:
        steps = jnp.exp(jax.random.uniform(jax.random.fold_in(own, dim), (parts,), jnp.float32, low / len(shards), top_value / len(shards)))
        gain = gain * jnp.repeat(steps, dims[dim] // parts).reshape([-1 if axis == dim else 1 for axis in range(len(dims))])
    return gain


def noise(rng, dims, deviation, limit, split=(), dtype=jnp.bfloat16):
    array = jax.random.normal(rng, dims, jnp.float32) * deviation
    if len(split) > 0:
        array = level_of(rng, dims, split, -0.22, 0.18) * array
    return jnp.clip(array, min=-limit, max=limit).astype(dtype)


def setup_inputs(seed: int = 0, part: int = 0) -> dict:
    keys = jax.random.split(jax.random.key(seed), 5)
    own_keys = jax.random.split(jax.random.fold_in(keys[4], part), 5)
    panel_data = noise(own_keys[0], (UNITS, PERIODS), 2.5, 12.0, ((0, 4), (1, 4)))
    observed = place_ends((jax.random.randint(own_keys[1], (UNITS, PERIODS), 0, 4) < 3).astype(jnp.int32), jax.random.fold_in(own_keys[1], 1), 0, 1)
    unit_factors = noise(own_keys[2], (UNITS, RANK), (RANK ** -0.25), 6.0, ((0, 16),), jnp.float32)
    period_factors = noise(own_keys[3], (PERIODS, RANK), (RANK ** -0.25), 6.0, ((0, 4),), jnp.float32)
    return {"panel_data": panel_data, "observed": observed, "unit_factors": unit_factors, "period_factors": period_factors}


def masked_residual(panel_data, observed, unit_half, period_half):
    fitted = lax.dot_general(unit_half, period_half, (((1,), (1,)), ((), ())), preferred_element_type=jnp.float32)
    return (observed.astype(jnp.float32) * (panel_data.astype(jnp.float32) - fitted)).astype(jnp.bfloat16)

def reference(panel_data, observed, unit_factors, period_factors):
    unit_rate = 0.5 * math.sqrt(RANK) / PERIODS
    period_rate = 0.5 * math.sqrt(RANK) / UNITS
    unit_full = unit_factors
    period_full = period_factors
    for iteration in range(ITERS):
        period_half = period_full.astype(jnp.bfloat16)
        residual = masked_residual(panel_data, observed, unit_full.astype(jnp.bfloat16), period_half)
        unit_full = unit_full + unit_rate * jnp.dot(residual, period_half, preferred_element_type=jnp.float32)
        unit_half = unit_full.astype(jnp.bfloat16)
        residual = masked_residual(panel_data, observed, unit_half, period_half)
        summed = lax.dot_general(residual, unit_half, (((0,), (0,)), ((), ())), preferred_element_type=jnp.float32)
        period_full = period_full + period_rate * summed
    return (unit_full, period_full)
```

```python
import functools
import math

import jax
import jax.numpy as jnp
from jax import lax
from jax.experimental import pallas as pl
from jax.experimental.pallas import tpu as pltpu
from jax.sharding import PartitionSpec as P

RANK = 32
ITERS = 2
F32, BF16 = jnp.float32, jnp.bfloat16
SHARE = ("period", "rep")
WHOLE = pl.BlockSpec(memory_space=pltpu.VMEM)


def swap_all(block, axes):
    size = lax.axis_size(axes)
    return [
        lax.ppermute(block, axes, [(i, i ^ step) for i in range(size)]) for step in range(1, size)
    ]


def tree_sum(refs):
    blocks = [ref[...].astype(F32) for ref in refs]
    while len(blocks) > 1:
        blocks = [a + b for a, b in zip(blocks[::2], blocks[1::2])]
    return blocks[0]


def masked_residual(units, periods, panel, mask):
    fitted = lax.dot_general(units, periods, (((0,), (0,)), ((), ())), preferred_element_type=F32)
    return (panel.astype(F32) - fitted).astype(BF16) * mask


def unit_partial(units, periods, panel, mask):
    residual = masked_residual(units, periods, panel, mask)
    return lax.dot_general(
        periods, residual, (((1,), (1,)), ((), ())), preferred_element_type=F32
    ).astype(BF16)


def first_unit_kernel(*refs):
    *shares, period, panel, observed, mask, unit, part, rows = refs
    me = lax.axis_index(SHARE)
    size = shares[0].shape[1]
    for step, share in enumerate(shares):
        rows[pl.ds((me ^ step) * size, size), :] = share[...].T
    whole = rows[...].T
    unit[...] = whole
    mask[...] = observed[...].astype(F32).astype(BF16)
    part[...] = unit_partial(
        whole.astype(BF16), period[...].astype(BF16), panel[...], mask[...]
    )


def period_kernel(rate, *refs):
    *parts, unit, period, panel, mask, new_unit, part = refs
    whole = unit[...] + rate * tree_sum(parts)
    new_unit[...] = whole
    units = whole.astype(BF16)
    residual = masked_residual(units, period[...].astype(BF16), panel[...], mask[...])
    part[...] = jnp.dot(units, residual, preferred_element_type=F32).astype(BF16)


def unit_kernel(rate, *refs):
    *parts, unit, period, panel, mask, new_period, part = refs
    whole = period[...] + rate * tree_sum(parts)
    new_period[...] = whole
    part[...] = unit_partial(
        unit[...].astype(BF16), whole.astype(BF16), panel[...], mask[...]
    )


def share_kernel(unit, share, rows):
    size = share.shape[1]
    rows[...] = unit[...].T
    share[...] = rows[pl.ds(lax.axis_index(SHARE) * size, size), :].T


def last_period_kernel(rate, *refs):
    *parts, period, new_period = refs
    new_period[...] = period[...] + rate * tree_sum(parts)


def call(kernel, outs, args, scratch=()):
    return pl.pallas_call(
        kernel,
        in_specs=[WHOLE] * len(args),
        out_specs=[WHOLE] * len(outs),
        out_shape=[jax.ShapeDtypeStruct(shape, dtype) for shape, dtype in outs],
        scratch_shapes=[pltpu.VMEM(shape, dtype) for shape, dtype in scratch],
        compiler_params=pltpu.CompilerParams(vmem_limit_bytes=24 * 2**20),
    )(*args)


def on_device(panel, observed, unit_factors, period_factors):
    units, periods = panel.shape
    unit_rate = 0.5 * math.sqrt(RANK) / (periods * lax.axis_size(SHARE))
    period_rate = 0.5 * math.sqrt(RANK) / (units * lax.axis_size("unit"))
    unit_like, period_like = (RANK, units), (RANK, periods)

    own = unit_factors.T
    period = period_factors.T
    mask, unit, part = call(
        first_unit_kernel,
        [(panel.shape, BF16), (unit_like, F32), (unit_like, BF16)],
        [own, *swap_all(own, SHARE), period, panel, observed],
        [((units, RANK), F32)],
    )
    for iteration in range(ITERS):
        unit, sums = call(
            functools.partial(period_kernel, unit_rate),
            [(unit_like, F32), (period_like, BF16)],
            [part, *swap_all(part, SHARE), unit, period, panel, mask],
        )
        if iteration < ITERS - 1:
            period, part = call(
                functools.partial(unit_kernel, period_rate),
                [(period_like, F32), (unit_like, BF16)],
                [sums, *swap_all(sums, "unit"), unit, period, panel, mask],
            )
    (share,) = call(share_kernel, [(own.shape, F32)], [unit], [((units, RANK), F32)])
    (period,) = call(
        functools.partial(last_period_kernel, period_rate),
        [(period_like, F32)],
        [sums, *swap_all(sums, "unit"), period],
    )
    return share.T, period.T


def solution(mesh):
    in_specs = (
        P(("grp", "unit"), ("period", "rep")),
        P(("grp", "unit"), ("period", "rep")),
        P(("grp", "unit", "period", "rep"), None),
        P(("grp", "period", "rep"), None),
    )
    out_specs = (P(("grp", "unit", "period", "rep"), None), P(("grp", "period", "rep"), None))
    return jax.shard_map(
        on_device, mesh=mesh, in_specs=in_specs, out_specs=out_specs, check_vma=False
    )
```

```python
import functools
import math

import jax
import jax.numpy as jnp
from jax import lax
from jax.experimental import pallas as pl
from jax.experimental.pallas import tpu as pltpu
from jax.sharding import PartitionSpec as P

RANK = 32
ITERS = 2
F32, BF16 = jnp.float32, jnp.bfloat16
SHARE = ("period", "rep")
SHARE_ORDER, UNIT_ORDER, PERIOD_ORDER = (0, 1, 2, 3), (0, 3, 1, 2), (0, 1, 3, 2)
WHOLE = pl.BlockSpec(memory_space=pltpu.VMEM)


def swap_all(block, axes, order=None):
    size = lax.axis_size(axes)
    blocks = [block] + [
        lax.ppermute(block, axes, [(i, i ^ step) for i in range(size)]) for step in range(1, size)
    ]
    return [blocks[step] for step in order] if order and size == len(order) else blocks


def unordered(refs, order):
    blocks = [ref[...] for ref in refs]
    if len(blocks) != len(order):
        return blocks
    return [blocks[order.index(step)] for step in range(len(order))]


def tree_sum(blocks):
    blocks = [block.astype(F32) for block in blocks]
    while len(blocks) > 1:
        blocks = [a + b for a, b in zip(blocks[::2], blocks[1::2])]
    return blocks[0]


def by_index(blocks):
    me = lax.axis_index(SHARE)
    bit = 1
    while bit < len(blocks):
        other = (me & bit) != 0
        blocks = [jnp.where(other, blocks[i ^ bit], block) for i, block in enumerate(blocks)]
        bit *= 2
    return blocks


def masked_residual(units, periods, panel, mask):
    fitted = lax.dot_general(units, periods, (((0,), (0,)), ((), ())), preferred_element_type=F32)
    return (panel.astype(F32) - fitted).astype(BF16) * mask


def unit_partial(units, periods, panel, mask):
    residual = masked_residual(units, periods, panel, mask)
    return lax.dot_general(
        periods, residual, (((1,), (1,)), ((), ())), preferred_element_type=F32
    ).astype(BF16)


def mask_kernel(observed, mask, raw, sems):
    pieces, size, _ = raw.shape
    loads = [
        pltpu.make_async_copy(observed.at[pl.ds(i * size, size), :], raw.at[i], sems.at[i])
        for i in range(pieces)
    ]
    for load in loads:
        load.start()
    for i, load in enumerate(loads):
        load.wait()
        mask[pl.ds(i * size, size), :] = raw[i].astype(F32).astype(BF16)


def mask_of(observed, pieces=4):
    units, periods = observed.shape
    return pl.pallas_call(
        mask_kernel,
        in_specs=[pl.BlockSpec(memory_space=pltpu.HBM)],
        out_specs=WHOLE,
        out_shape=jax.ShapeDtypeStruct(observed.shape, BF16),
        scratch_shapes=[
            pltpu.VMEM((pieces, units // pieces, periods), observed.dtype),
            pltpu.SemaphoreType.DMA((pieces,)),
        ],
        compiler_params=pltpu.CompilerParams(vmem_limit_bytes=50 * 2**20),
        cost_estimate=pl.CostEstimate(
            flops=2 * units * periods, bytes_accessed=6 * units * periods, transcendentals=0
        ),
    )(observed)


def first_unit_kernel(*refs):
    *shares, period, panel, mask, unit, part = refs
    size = shares[0].shape[1]
    for place, share in enumerate(by_index(unordered(shares, SHARE_ORDER))):
        unit[:, place * size : (place + 1) * size] = share
    whole = unit[...]
    part[...] = unit_partial(
        whole.astype(BF16), period[...].astype(BF16), panel[...], mask[...]
    )


def period_kernel(rate, *refs):
    *parts, unit, period, panel, mask, new_unit, part = refs
    whole = unit[...] + rate * tree_sum(unordered(parts, UNIT_ORDER))
    new_unit[...] = whole
    units = whole.astype(BF16)
    residual = masked_residual(units, period[...].astype(BF16), panel[...], mask[...])
    part[...] = jnp.dot(units, residual, preferred_element_type=F32).astype(BF16)


def unit_kernel(rate, *refs):
    *parts, unit, period, panel, mask, new_period, part = refs
    whole = period[...] + rate * tree_sum(unordered(parts, PERIOD_ORDER))
    new_period[...] = whole
    part[...] = unit_partial(
        unit[...].astype(BF16), whole.astype(BF16), panel[...], mask[...]
    )


def share_kernel(unit, share):
    size = share.shape[1]
    count = unit.shape[1] // size
    share[...] = by_index([unit[:, i * size : (i + 1) * size] for i in range(count)])[0]


def last_period_kernel(rate, *refs):
    *parts, period, new_period = refs
    new_period[...] = period[...] + rate * tree_sum(unordered(parts, PERIOD_ORDER))


def call(kernel, outs, args, scratch=()):
    return pl.pallas_call(
        kernel,
        in_specs=[WHOLE] * len(args),
        out_specs=[WHOLE] * len(outs),
        out_shape=[jax.ShapeDtypeStruct(shape, dtype) for shape, dtype in outs],
        scratch_shapes=[pltpu.VMEM(shape, dtype) for shape, dtype in scratch],
        compiler_params=pltpu.CompilerParams(vmem_limit_bytes=24 * 2**20),
    )(*args)


def on_device(panel, observed, unit_factors, period_factors):
    units, periods = panel.shape
    unit_rate = 0.5 * math.sqrt(RANK) / (periods * lax.axis_size(SHARE))
    period_rate = 0.5 * math.sqrt(RANK) / (units * lax.axis_size("unit"))
    unit_like, period_like = (RANK, units), (RANK, periods)

    own = unit_factors.T
    mask = mask_of(observed)
    period = period_factors.T
    unit, part = call(
        first_unit_kernel,
        [(unit_like, F32), (unit_like, BF16)],
        [*swap_all(own, SHARE, SHARE_ORDER), period, panel, mask],
    )
    for iteration in range(ITERS):
        unit, sums = call(
            functools.partial(period_kernel, unit_rate),
            [(unit_like, F32), (period_like, BF16)],
            [*swap_all(part, SHARE, UNIT_ORDER), unit, period, panel, mask],
        )
        if iteration < ITERS - 1:
            period, part = call(
                functools.partial(unit_kernel, period_rate),
                [(period_like, F32), (unit_like, BF16)],
                [*swap_all(sums, "unit", PERIOD_ORDER), unit, period, panel, mask],
            )
    (share,) = call(share_kernel, [(own.shape, F32)], [unit])
    (period,) = call(
        functools.partial(last_period_kernel, period_rate),
        [(period_like, F32)],
        [*swap_all(sums, "unit", PERIOD_ORDER), period],
    )
    return share.T, period.T


def solution(mesh):
    in_specs = (
        P(("grp", "unit"), ("period", "rep")),
        P(("grp", "unit"), ("period", "rep")),
        P(("grp", "unit", "period", "rep"), None),
        P(("grp", "period", "rep"), None),
    )
    out_specs = (P(("grp", "unit", "period", "rep"), None), P(("grp", "period", "rep"), None))
    return jax.shard_map(
        on_device, mesh=mesh, in_specs=in_specs, out_specs=out_specs, check_vma=False
    )
```

```python
import functools
import math

import jax
import jax.numpy as jnp
from jax import lax
from jax.experimental import pallas as pl
from jax.experimental.pallas import tpu as pltpu
from jax.sharding import PartitionSpec as P

RANK = 32
ITERS = 2
F32, BF16 = jnp.float32, jnp.bfloat16
SHARE = ("period", "rep")
UNIT_ORDER, PERIOD_ORDER = (0, 1, 3, 2), (0, 1, 3, 2)
WHOLE = pl.BlockSpec(memory_space=pltpu.VMEM)


def swap_all(block, axes, order=None):
    size = lax.axis_size(axes)
    blocks = [block] + [
        lax.ppermute(block, axes, [(i, i ^ step) for i in range(size)]) for step in range(1, size)
    ]
    return [blocks[step] for step in order] if order and size == len(order) else blocks


def unordered(refs, order):
    blocks = [ref[...] for ref in refs]
    if len(blocks) != len(order):
        return blocks
    return [blocks[order.index(step)] for step in range(len(order))]


def tree_sum(blocks):
    blocks = [block.astype(F32) for block in blocks]
    while len(blocks) > 1:
        blocks = [a + b for a, b in zip(blocks[::2], blocks[1::2])]
    return blocks[0]


def by_index(blocks, axis):
    me = lax.axis_index(axis)
    bit = 1
    while bit < len(blocks):
        other = (me & bit) != 0
        blocks = [jnp.where(other, blocks[i ^ bit], block) for i, block in enumerate(blocks)]
        bit *= 2
    return blocks


def lay_out(target, blocks):
    size = blocks[0].shape[1]
    for place, block in enumerate(blocks):
        target[:, place * size : (place + 1) * size] = block


def masked_residual(units, periods, panel, mask):
    fitted = lax.dot_general(units, periods, (((0,), (0,)), ((), ())), preferred_element_type=F32)
    return (panel.astype(F32) - fitted).astype(BF16) * mask


def unit_partial(units, periods, panel, mask):
    residual = masked_residual(units, periods, panel, mask)
    return lax.dot_general(
        periods, residual, (((1,), (1,)), ((), ())), preferred_element_type=F32
    ).astype(BF16)


def mask_kernel(observed, mask, raw, sems):
    pieces, size, _ = raw.shape
    loads = [
        pltpu.make_async_copy(observed.at[pl.ds(i * size, size), :], raw.at[i], sems.at[i])
        for i in range(pieces)
    ]
    for load in loads:
        load.start()
    for i, load in enumerate(loads):
        load.wait()
        mask[pl.ds(i * size, size), :] = raw[i].astype(F32).astype(BF16)


def mask_of(observed, pieces=4):
    units, periods = observed.shape
    return pl.pallas_call(
        mask_kernel,
        in_specs=[pl.BlockSpec(memory_space=pltpu.HBM)],
        out_specs=WHOLE,
        out_shape=jax.ShapeDtypeStruct(observed.shape, BF16),
        scratch_shapes=[
            pltpu.VMEM((pieces, units // pieces, periods), observed.dtype),
            pltpu.SemaphoreType.DMA((pieces,)),
        ],
        compiler_params=pltpu.CompilerParams(vmem_limit_bytes=50 * 2**20),
        cost_estimate=pl.CostEstimate(
            flops=2 * units * periods, bytes_accessed=6 * units * periods, transcendentals=0
        ),
    )(observed)


def chip_units(shares, step, unit, period, panel, mask):
    lay_out(unit, by_index([share[...] for share in shares], "rep"))
    size = unit.shape[1]
    rows = pl.ds(pl.multiple_of((lax.axis_index("period") ^ step) * size, 16), size)
    return unit_partial(
        unit[...].astype(BF16), period[...].astype(BF16), panel[rows, :], mask[rows, :]
    )


def own_unit_kernel(share, other, period, panel, mask, unit, part):
    part[...] = chip_units([share, other], 0, unit, period, panel, mask)


def first_unit_kernel(*refs):
    *shares, own_unit, own_part, period, panel, mask, unit, part, chips = refs
    shares = shares[::-1]
    units, parts = [own_unit[...]], [own_part[...]]
    for step in range(1, chips.shape[0] + 1):
        pair = shares[2 * step - 2 : 2 * step]
        parts.append(chip_units(pair, step, chips.at[step - 1], period, panel, mask))
        units.append(chips[step - 1])
    lay_out(unit, by_index(units, "period"))
    lay_out(part, by_index(parts, "period"))


def period_kernel(rate, *refs):
    *parts, unit, period, panel, mask, new_unit, part = refs
    whole = unit[...] + rate * tree_sum(unordered(parts, UNIT_ORDER))
    new_unit[...] = whole
    units = whole.astype(BF16)
    residual = masked_residual(units, period[...].astype(BF16), panel[...], mask[...])
    part[...] = jnp.dot(units, residual, preferred_element_type=F32).astype(BF16)


def unit_kernel(rate, *refs):
    *parts, unit, period, panel, mask, new_period, part = refs
    whole = period[...] + rate * tree_sum(unordered(parts, PERIOD_ORDER))
    new_period[...] = whole
    part[...] = unit_partial(
        unit[...].astype(BF16), whole.astype(BF16), panel[...], mask[...]
    )


def share_kernel(unit, share):
    size = share.shape[1]
    count = unit.shape[1] // size
    blocks = [unit[:, i * size : (i + 1) * size] for i in range(count)]
    share[...] = by_index(blocks, SHARE)[0]


def last_period_kernel(rate, *refs):
    *parts, period, new_period = refs
    new_period[...] = period[...] + rate * tree_sum(unordered(parts, PERIOD_ORDER))


def call(kernel, outs, args, scratch=()):
    return pl.pallas_call(
        kernel,
        in_specs=[WHOLE] * len(args),
        out_specs=[WHOLE] * len(outs),
        out_shape=[jax.ShapeDtypeStruct(shape, dtype) for shape, dtype in outs],
        scratch_shapes=[pltpu.VMEM(shape, dtype) for shape, dtype in scratch],
        compiler_params=pltpu.CompilerParams(vmem_limit_bytes=24 * 2**20),
    )(*args)


def on_device(panel, observed, unit_factors, period_factors):
    units, periods = panel.shape
    unit_rate = 0.5 * math.sqrt(RANK) / (periods * lax.axis_size(SHARE))
    period_rate = 0.5 * math.sqrt(RANK) / (units * lax.axis_size("unit"))
    unit_like, period_like = (RANK, units), (RANK, periods)

    own = unit_factors.T
    mask = mask_of(observed)
    period = period_factors.T
    shares = swap_all(own, SHARE)
    chip_like = (RANK, 2 * own.shape[1])
    unit, part = call(
        own_unit_kernel,
        [(chip_like, F32), (chip_like, BF16)],
        [*shares[:2], period, panel, mask],
    )
    unit, part = call(
        first_unit_kernel,
        [(unit_like, F32), (unit_like, BF16)],
        [*shares[:1:-1], unit, part, period, panel, mask],
        [((units // chip_like[1] - 1, *chip_like), F32)],
    )
    for iteration in range(ITERS):
        unit, sums = call(
            functools.partial(period_kernel, unit_rate),
            [(unit_like, F32), (period_like, BF16)],
            [*swap_all(part, SHARE, UNIT_ORDER), unit, period, panel, mask],
        )
        if iteration < ITERS - 1:
            period, part = call(
                functools.partial(unit_kernel, period_rate),
                [(period_like, F32), (unit_like, BF16)],
                [*swap_all(sums, "unit", PERIOD_ORDER), unit, period, panel, mask],
            )
    (share,) = call(share_kernel, [(own.shape, F32)], [unit])
    (period,) = call(
        functools.partial(last_period_kernel, period_rate),
        [(period_like, F32)],
        [*swap_all(sums, "unit", PERIOD_ORDER), period],
    )
    return share.T, period.T


def solution(mesh):
    in_specs = (
        P(("grp", "unit"), ("period", "rep")),
        P(("grp", "unit"), ("period", "rep")),
        P(("grp", "unit", "period", "rep"), None),
        P(("grp", "period", "rep"), None),
    )
    out_specs = (P(("grp", "unit", "period", "rep"), None), P(("grp", "period", "rep"), None))
    return jax.shard_map(
        on_device, mesh=mesh, in_specs=in_specs, out_specs=out_specs, check_vma=False
    )
```
